128 devices in a mesh: dp: 16 (over x_hi, y, core), expert: 8 (over z, x_lo).
Axes of the slice: x: 4 (x_hi: 2, x_lo: 2; x = x_hi * 2 + x_lo), y: 4, z: 4, core: 2. Of those that a mesh axis runs over, the one named last changes fastest.
Arguments:
- expert_partials: float32 [16, 8, 1536, 2048], P('dp', 'expert'), may hold values from -5 to 5
- key_partials: float32 [16, 512, 4096], P('dp', None, 'expert'), may hold values from -5 to 5
- expert_param: float32 [8, 1536, 2048], P('expert', 'dp'), may hold values from -0.3125 to 0.3125
- expert_moment: float32 [8, 1536, 2048], P('expert', 'dp'), may hold values from -4 to 4
- expert_second: float32 [8, 1536, 2048], P('expert', 'dp'), may hold values from 0.05 to 1
- key_param: float32 [512, 4096], P('dp', 'expert'), may hold values from -0.3125 to 0.3125
- key_moment: float32 [512, 4096], P('dp', 'expert'), may hold values from -4 to 4
- key_second: float32 [512, 4096], P('dp', 'expert'), may hold values from 0.05 to 1
- expert_scales: float32 [8, 12, 16], replicated, may hold values from 0.0001 to 0.001
- key_scales: float32 [4, 32], P(None, 'expert'), may hold values from 0.0001 to 0.001
- rotary_order: int32 [128], replicated, may hold values from 0 to 127, each once
- expert_slot: int32 [8], replicated, may hold values from 0 to 7, each once
Outputs:
- new_expert_param: float32 [8, 1536, 2048], P('expert', 'dp')
- new_expert_moment: float32 [8, 1536, 2048], P('expert', 'dp')
- new_expert_second: float32 [8, 1536, 2048], P('expert', 'dp')
- new_key_param: float32 [512, 4096], P('dp', 'expert')
- new_key_moment: float32 [512, 4096], P('dp', 'expert')
- new_key_second: float32 [512, 4096], P('dp', 'expert')
- server_expert: bfloat16 [8, 2048, 1536], P(None, 'expert', 'dp')
- server_key: bfloat16 [4096, 512], P('expert')
The draws below stay inside these ranges and needn't reach their ends.
Inputs may be any that keep to these rules, and one draw needn't show every extreme that they name: `rotary_order`: a permutation of the rows of one head. `expert_slot`: a permutation of the experts.
All inputs are finite; a program needn't handle non-finite values.
Results may differ from the reference program's by a relative error of at most 0.007.
Values may be sent and summed in bfloat16 or wider, within the bound.
No kernel may reach another device: no remote copies, remote signals or barrier semaphores. Data moves between devices by JAX's collectives and lax.ppermute only.
A program may use at most 128 MiB of HBM per device.

```python
import math
import jax
import jax.numpy as jnp
from jax import lax

D = 4096
DW = 2048
FW = 1536
HD = 128
BLOCK = 128
EXPERTS = 8
KR = 512
N_DP = 16


def strengthened(values, rng, source, target, parts, factor):
    def block_of(dim):
        return (jnp.arange(values.shape[dim]) // (values.shape[dim] // parts)).reshape((-1,) + (1,) * (values.ndim - 1 - dim))

    near = jax.random.permutation(rng, parts)[block_of(target)]
    second = (block_of(target) + parts // 2) % parts
    return jnp.where((block_of(source) == near) | (block_of(source) == second), factor * values, values)


def block_levels(own_key, dims, shards, smallest, high):
    gain = 1.0
    for position, blocks in shards:
        draws = jax.random.uniform(jax.random.fold_in(jax.random.fold_in(own_key, 6), position), (blocks,), jnp.float32, smallest / len(shards), high / len(shards))
        gain = gain * jnp.repeat(jnp.exp(draws), dims[position] // blocks).reshape((-1,) + (1,) * (len(dims) - 1 - position))
    return gain


def normal_values(stream_key, shape, spread, limit, shards=(), held_as=jnp.bfloat16):
    array = spread * jax.random.normal(stream_key, shape, jnp.float32)
    if shards:
        array = array * block_levels(stream_key, shape, shards, -0.22, 0.18)
    return jnp.clip(array, -limit, limit).astype(held_as)


def noise_with(key, extent, spread, bound, split, heavy, kind=jnp.bfloat16):
    result = spread * jax.random.normal(key, extent, jnp.float32)
    if split:
        result = result * block_levels(key, extent, split, -0.22, 0.18)
    return jnp.clip(strengthened(result, jax.random.fold_in(key, 3), *heavy), -bound, bound).astype(kind)


def setup_inputs(seed: int = 0) -> dict:
    arg_keys = jax.random.split(jax.random.key(seed), 13)
    expert_partials = noise_with(arg_keys[0], (N_DP, EXPERTS, FW, DW), 0.25, 5.0, ((0, 16), (1, 8)), (0, 2, 16, 2.0), jnp.float32)
    key_partials = noise_with(arg_keys[1], (N_DP, KR, D), 0.25, 5.0, ((0, 16), (2, 8)), (0, 1, 16, 2.0), jnp.float32)
    expert_param = normal_values(arg_keys[2], (EXPERTS, FW, DW), 0.02, 0.3125, ((0, 8), (1, 16)), jnp.float32)
    expert_moment = normal_values(arg_keys[3], (EXPERTS, FW, DW), 0.3, 4.0, ((0, 8), (1, 16)), jnp.float32)
    expert_second = jnp.clip(jnp.exp(math.log(1.0) - 2.9957323 * jax.random.uniform(arg_keys[4], (EXPERTS, FW, DW), jnp.float32) ** block_levels(arg_keys[4], (EXPERTS, FW, DW), ((0, 8), (1, 16)), -0.2, 0.2)), 0.05, 1.0)
    key_param = normal_values(arg_keys[5], (KR, D), 0.02, 0.3125, ((0, 16), (1, 8)), jnp.float32)
    key_moment = normal_values(arg_keys[6], (KR, D), 0.3, 4.0, ((0, 16), (1, 8)), jnp.float32)
    key_second = jnp.clip(jnp.exp(math.log(1.0) - 2.9957323 * jax.random.uniform(arg_keys[7], (KR, D), jnp.float32) ** block_levels(arg_keys[7], (KR, D), ((0, 16), (1, 8)), -0.2, 0.2)), 0.05, 1.0)
    expert_scales = jnp.clip(jnp.exp(jax.random.uniform(arg_keys[8], (EXPERTS, FW // BLOCK, DW // BLOCK), jnp.float32, math.log(0.0001), math.log(0.001))), 0.0001, 0.001)
    key_scales = jnp.clip(jnp.exp(math.log(0.001) - 2.3025852 * jax.random.uniform(arg_keys[9], (KR // BLOCK, D // BLOCK), jnp.float32) ** block_levels(arg_keys[9], (KR // BLOCK, D // BLOCK), ((1, 8),), -0.2, 0.2)), 0.0001, 0.001)
    rotary_order = jax.random.permutation(arg_keys[10], HD).astype(jnp.int32)
    expert_slot = jax.random.permutation(arg_keys[11], EXPERTS).astype(jnp.int32)
    return {"expert_partials": expert_partials, "key_partials": key_partials, "expert_param": expert_param, "expert_moment": expert_moment, "expert_second": expert_second, "key_param": key_param, "key_moment": key_moment, "key_second": key_second, "expert_scales": expert_scales, "key_scales": key_scales, "rotary_order": rotary_order, "expert_slot": expert_slot}


BETA_ONE = 0.9
BETA_TWO = 0.95
LEARN = 0.01
DECAY = 0.1
EPSILON = 1e-08
LIMIT = 448.0
CORRECT_ONE = 1.0 - 0.9 ** 10
CORRECT_TWO = 1.0 - 0.95 ** 10

def adam_update(param, moment, second, grad):
    moment = BETA_ONE * moment + (1.0 - BETA_ONE) * grad
    second = BETA_TWO * second + (1.0 - BETA_TWO) * grad * grad
    corrected = moment / CORRECT_ONE / (jnp.sqrt(second / CORRECT_TWO) + EPSILON)
    return (param * (1.0 - LEARN * DECAY) - LEARN * corrected, moment, second)

def to_grid(weights, scales):
    return jnp.clip(weights / scales, -LIMIT, LIMIT).astype(jnp.bfloat16)

def reference(expert_partials, key_partials, expert_param, expert_moment, expert_second, key_param, key_moment, key_second, expert_scales, key_scales, rotary_order, expert_slot):
    expert_grad = lax.optimization_barrier(jnp.sum(expert_partials, axis=0))
    key_grad = lax.optimization_barrier(jnp.sum(key_partials, axis=0))
    new_ep, new_em, new_es = adam_update(expert_param, expert_moment, expert_second, expert_grad)
    new_kp, new_km, new_ks = adam_update(key_param, key_moment, key_second, key_grad)
    full_expert = jnp.repeat(jnp.repeat(expert_scales, BLOCK, axis=1), BLOCK, axis=2)
    expert_grid = to_grid(new_ep, full_expert)
    server_expert = jnp.zeros((EXPERTS, DW, FW), jnp.bfloat16).at[expert_slot].set(jnp.transpose(expert_grid, (0, 2, 1)))
    full_key = jnp.repeat(jnp.repeat(key_scales, BLOCK, axis=0), BLOCK, axis=1)
    key_grid = to_grid(new_kp, full_key)
    rows = jnp.arange(KR, dtype=jnp.int32)
    source = rows // HD * HD + rotary_order[rows % HD]
    server_key = jnp.take(key_grid, source, axis=0).T
    return (new_ep, new_em, new_es, new_kp, new_km, new_ks, server_expert, server_key)
```

```python
import functools

import jax
import jax.numpy as jnp
from jax import lax
from jax.experimental import pallas as pl
from jax.experimental.pallas import tpu as pltpu
from jax.sharding import PartitionSpec as P

HD = 128
BLOCK = 128

BETA_ONE = 0.9
BETA_TWO = 0.95
LEARN = 0.01
DECAY = 0.1
EPSILON = 1e-08
LIMIT = 448.0
CORRECT_ONE = 1.0 - 0.9**10
CORRECT_TWO = 1.0 - 0.95**10

ROWS = 96
KROWS = 32
HALF = 1024
KCOLS = 512
PROWS = 112

BF = jnp.bfloat16
F32 = jnp.float32
VMEM_BYTES = 40 * 1024 * 1024


def dp_of(x, y, c):
    return ((x % 2) * 4 + (y % 4)) * 2 + c % 2


def dp_perm(dx, dy, dc):
    return [
        (dp_of(x, y, c), dp_of(x + dx, y + dy, c + dc))
        for x in range(2)
        for y in range(4)
        for c in range(2)
    ]


def send(value, dx, dy, dc):
    return lax.ppermute(value, "dp", dp_perm(dx, dy, dc))


def adam_update(param, moment, second, grad):
    moment = BETA_ONE * moment + (1.0 - BETA_ONE) * grad
    second = BETA_TWO * second + (1.0 - BETA_TWO) * grad * grad
    corrected = moment / CORRECT_ONE / (jnp.sqrt(second / CORRECT_TWO) + EPSILON)
    return (param * (1.0 - LEARN * DECAY) - LEARN * corrected, moment, second)


def to_grid(weights, scales):
    return jnp.clip(weights / scales, -LIMIT, LIMIT).astype(BF)


def stage_kernel(pieces, received_at, written_at, n_received, ids, ep, kp, *refs):
    received = refs[:n_received]
    n_out = 1 + max(place[0] for place in written_at)
    outs = refs[n_received : n_received + n_out]
    ebuf, kbuf, esem, ksem = refs[n_received + n_out :]
    copies = []
    kslot = 0
    for slot, (kind, _, _) in enumerate(pieces):
        half = 0 if kind == "P" else 1
        block = ids[slot]
        one = pltpu.make_async_copy(
            ep.at[block, :, pl.ds(half * HALF, HALF)], ebuf.at[slot], esem.at[slot]
        )
        one.start()
        two = None
        if kind == "P":
            two = pltpu.make_async_copy(kp.at[block], kbuf.at[kslot], ksem.at[kslot])
            two.start()
        copies.append((one, two, kslot))
        kslot += kind == "P"
    for slot, (kind, _, _) in enumerate(pieces):
        one, two, kslot = copies[slot]
        out, place = outs[written_at[slot][0]], written_at[slot][1]
        one.wait()
        value = ebuf[slot]
        if n_received:
            group, index = received_at[slot]
            value = value + received[group][index, 0:ROWS].astype(F32)
        out[place, 0:ROWS] = value.astype(BF)
        if two is not None:
            two.wait()
            for part in range(2):
                value = kbuf[kslot, part * 16 : part * 16 + 16]
                if n_received:
                    value = value + received[group][
                        index, ROWS:PROWS, part * KCOLS : (part + 1) * KCOLS
                    ].astype(F32)
                out[place, ROWS:PROWS, part * KCOLS : (part + 1) * KCOLS] = value.astype(BF)


def stage(ids, ep, kp, groups, received=(), received_at=None):
    pieces, written_at, shapes = [], [], []
    for number, group in enumerate(groups):
        for place, piece in enumerate(group):
            pieces.append(piece)
            written_at.append((number, place))
        rows = PROWS if group[0][0] == "P" else ROWS
        shapes.append(pltpu.VMEM((len(group), rows, HALF), BF))
    n_key = max(1, sum(piece[0] == "P" for piece in pieces))
    x, y, c = ids
    blocks = jnp.stack([dp_of(x + dx, y + dy, c) for _, dx, dy in pieces]).astype(jnp.int32)
    vmem = pl.BlockSpec(memory_space=pltpu.VMEM)
    hbm = pl.BlockSpec(memory_space=pl.ANY)
    return pl.pallas_call(
        functools.partial(stage_kernel, pieces, received_at, written_at, len(received)),
        out_shape=shapes,
        in_specs=[pl.BlockSpec(memory_space=pltpu.SMEM), hbm, hbm] + [vmem] * len(received),
        out_specs=[vmem] * len(shapes),
        scratch_shapes=[
            pltpu.VMEM((len(pieces), ROWS, HALF), F32),
            pltpu.VMEM((n_key, KROWS, KCOLS), F32),
            pltpu.SemaphoreType.DMA((len(pieces),)),
            pltpu.SemaphoreType.DMA((n_key,)),
        ],
        compiler_params=pltpu.CompilerParams(vmem_limit_bytes=VMEM_BYTES),
        cost_estimate=pl.CostEstimate(
            flops=len(pieces) * ROWS * HALF,
            bytes_accessed=len(pieces) * ROWS * HALF * 6,
            transcendentals=0,
        ),
    )(blocks, ep, kp, *received)


def plus(*values):
    total = values[0].astype(F32)
    for value in values[1:]:
        total = total + value.astype(F32)
    return total


def turn_kernel(slot, arrived, out):
    del slot
    out[0] = arrived[0].T


def turned(arrived, expert_slot):
    experts, rows, columns = arrived.shape
    return pl.pallas_call(
        turn_kernel,
        out_shape=jax.ShapeDtypeStruct((experts, columns, rows), BF),
        grid_spec=pltpu.PrefetchScalarGridSpec(
            num_scalar_prefetch=1,
            grid=(experts,),
            in_specs=[pl.BlockSpec((1, rows, columns), lambda e, slot: (e, 0, 0))],
            out_specs=pl.BlockSpec((1, columns, rows), lambda e, slot: (slot[e], 0, 0)),
        ),
    )(expert_slot, arrived)


def on_device(
    expert_partials,
    key_partials,
    expert_param,
    expert_moment,
    expert_second,
    key_param,
    key_moment,
    key_second,
    expert_scales,
    key_scales,
    rotary_order,
    expert_slot,
):
    dp_index = lax.axis_index("dp")
    expert_index = lax.axis_index("expert")
    x, y, c = dp_index // 8, dp_index // 2 % 4, dp_index % 2
    ep = expert_partials.reshape(16, ROWS, 2 * HALF)
    kp = key_partials.reshape(16, KROWS, KCOLS)
    mine, other = (x, y, c), (x, y, c + 1)

    group_a = [("P", 0, 2), ("P", 1, 2)]
    group_b = [("Q", 1, 2), ("Q", 1, 1), ("Q", 1, 3), ("Q", 1, 0)]
    group_c = [("P", 0, 1), ("P", 1, 1), ("P", 0, 3), ("P", 1, 3)]
    group_d = [("P", 0, 0), ("P", 1, 0)]
    group_e = [("Q", 0, 2), ("Q", 0, 1), ("Q", 0, 3), ("Q", 0, 0)]
    cast_a, cast_b = stage(other, ep, kp, [group_a, group_b])
    core_a, core_b = send(cast_a, 0, 0, 1), send(cast_b, 0, 0, 1)
    cast_c, cast_d, cast_e = stage(other, ep, kp, [group_c, group_d, group_e])
    core_c, core_d, core_e = (send(v, 0, 0, 1) for v in (cast_c, cast_d, cast_e))
    a0, a1 = stage(mine, ep, kp, [group_a[:1], group_a[1:]], (core_a,), [(0, 0), (0, 1)])
    up = send(a0, 0, 1, 0)
    down = send(a1, 0, -1, 0)
    b_far, b_rest = stage(
        mine, ep, kp, [group_b[:1], group_b[1:]], (core_b,), [(0, i) for i in range(4)]
    )
    x_far = send(b_far, 1, 0, 0)
    x_rest = send(b_rest, 1, 0, 0)
    c01, c11, c03, c13 = stage(
        mine, ep, kp, [[piece] for piece in group_c], (core_c,), [(0, i) for i in range(4)]
    )
    up_plain = send(c11, 0, 1, 0)
    down_plain = send(c03, 0, -1, 0)
    d0, d1, e2, e1, e3, e0 = stage(
        mine,
        ep,
        kp,
        [[piece] for piece in group_d + group_e],
        (core_d, core_e),
        [(0, 0), (0, 1)] + [(1, i) for i in range(4)],
    )
    up_sum = send(plus(c01, up).astype(BF), 0, 1, 0)
    down_sum = send(plus(c13, down).astype(BF), 0, -1, 0)
    q2 = plus(e2, x_far).astype(BF)
    q_up = send(q2[:, :48], 0, 1, 0)
    q_down = send(q2[:, 48:], 0, -1, 0)
    q1 = plus(e1, x_rest[0:1])
    q3 = plus(e3, x_rest[1:2])
    q0 = plus(e0, x_rest[2:3])
    q1 = jnp.concatenate([q1[:, :48] + q_up.astype(F32), q1[:, 48:]], axis=1).astype(BF)
    q3 = jnp.concatenate([q3[:, :48], q3[:, 48:] + q_down.astype(F32)], axis=1).astype(BF)
    x_last = send(plus(d1, up_plain, down_sum).astype(BF), 1, 0, 0)
    q_up_sum = send(q1, 0, 1, 0)
    q_down_sum = send(q3, 0, -1, 0)
    first = plus(d0, up_sum, down_plain, x_last)[0]
    second = (q0 + q_up_sum.astype(F32) + q_down_sum.astype(F32))[0]

    key_grad = jnp.concatenate([first[ROWS:, :KCOLS], first[ROWS:, KCOLS:]], axis=0)
    new_kp, new_km, new_ks = adam_update(key_param, key_moment, key_second, key_grad)
    key_row = lax.dynamic_slice_in_dim(key_scales, dp_index // 4, 1, 0)
    key_grid = to_grid(new_kp, jnp.repeat(key_row, BLOCK, axis=1))
    chip_x = send(key_grid, 1, 0, 0)
    column = jnp.stack([key_grid, chip_x])
    all_y = jnp.stack([column, send(column, 0, -1, 0), send(column, 0, -2, 0), send(column, 0, -3, 0)])
    everything = jnp.stack([all_y, send(all_y, 0, 0, 1)]).reshape(16 * KROWS, KCOLS)
    order = jnp.arange(16 * KROWS, dtype=jnp.int32)
    piece, row = order // KROWS, order % KROWS
    held = dp_of(x + piece % 2, y + piece // 2 % 4, c + piece // 8) * KROWS + row
    source = order // HD * HD + rotary_order[order % HD]
    pick = (held[:, None] == source[None, :]).astype(BF)
    server_key = lax.dot_general(
        everything, pick, (((0,), (0,)), ((), ())), preferred_element_type=F32
    ).astype(BF)

    expert_grad = jnp.concatenate([first[:ROWS], second], axis=1)
    new_ep, new_em, new_es = adam_update(expert_param, expert_moment, expert_second, expert_grad[None])
    row_blocks = (dp_index * ROWS + jnp.arange(ROWS, dtype=jnp.int32)) // BLOCK
    my_scales = lax.dynamic_index_in_dim(expert_scales, expert_index, 0, keepdims=False)
    row_scales = jnp.take(my_scales, row_blocks, axis=0)
    grid = to_grid(new_ep[0], jnp.repeat(row_scales, BLOCK, axis=1))
    blocks = jnp.transpose(grid.reshape(ROWS, 8, 256), (1, 0, 2))
    arrived = lax.all_to_all(blocks, "expert", split_axis=0, concat_axis=0, tiled=True)
    server_expert = turned(arrived, expert_slot)
    return (new_ep, new_em, new_es, new_kp, new_km, new_ks, server_expert, server_key)


def solution(mesh):
    return jax.shard_map(
        on_device,
        mesh=mesh,
        in_specs=(
            P("dp", "expert", None, None),
            P("dp", None, "expert"),
            P("expert", "dp", None),
            P("expert", "dp", None),
            P("expert", "dp", None),
            P("dp", "expert"),
            P("dp", "expert"),
            P("dp", "expert"),
            P(),
            P(None, "expert"),
            P(),
            P(),
        ),
        out_specs=(
            P("expert", "dp", None),
            P("expert", "dp", None),
            P("expert", "dp", None),
            P("dp", "expert"),
            P("dp", "expert"),
            P("dp", "expert"),
            P(None, "expert", "dp"),
            P("expert", None),
        ),
        check_vma=False,
    )
```

```python
import functools

import jax
import jax.numpy as jnp
from jax import lax
from jax.experimental import pallas as pl
from jax.experimental.pallas import tpu as pltpu
from jax.sharding import PartitionSpec as P

HD = 128
BLOCK = 128

BETA_ONE = 0.9
BETA_TWO = 0.95
LEARN = 0.01
DECAY = 0.1
EPSILON = 1e-08
LIMIT = 448.0
CORRECT_ONE = 1.0 - 0.9**10
CORRECT_TWO = 1.0 - 0.95**10

ROWS = 96
KROWS = 32
HALF = 1024
KCOLS = 512
PROWS = 112

BF = jnp.bfloat16
F32 = jnp.float32
VMEM_BYTES = 12 * 1024 * 1024


def dp_of(x, y, c):
    return ((x % 2) * 4 + (y % 4)) * 2 + c % 2


def dp_perm(dx, dy, dc):
    return [
        (dp_of(x, y, c), dp_of(x + dx, y + dy, c + dc))
        for x in range(2)
        for y in range(4)
        for c in range(2)
    ]


def send(value, dx, dy, dc):
    return lax.ppermute(value, "dp", dp_perm(dx, dy, dc))


def ring(value):
    pairs = [
        (dp_of(x, y, c), dp_of(x, y + 1 - 2 * c, c))
        for x in range(2)
        for y in range(4)
        for c in range(2)
    ]
    return lax.ppermute(value, "dp", pairs)


def after(value, *earlier):
    return lax.optimization_barrier((value, *earlier))[0]


def adam_update(param, moment, second, grad):
    moment = BETA_ONE * moment + (1.0 - BETA_ONE) * grad
    second = BETA_TWO * second + (1.0 - BETA_TWO) * grad * grad
    corrected = moment / CORRECT_ONE / (jnp.sqrt(second / CORRECT_TWO) + EPSILON)
    return (param * (1.0 - LEARN * DECAY) - LEARN * corrected, moment, second)


def to_grid(weights, scales):
    return jnp.clip(weights / scales, -LIMIT, LIMIT).astype(BF)


def owner(piece, x, y, c):
    _, dx, role = piece
    step = {"far": 2, "near": 1 - 2 * c, "plain": 1 - 2 * c, "own": 0}[role]
    return dp_of(x + dx, y + 4 + step, 1 - c if role == "plain" else c)


def parts_of(piece, block, ep, kp, out):
    if piece[0] == "Q":
        return [(ep.at[block, :, pl.ds(HALF, HALF)], out)]
    return [
        (ep.at[block, :, pl.ds(0, HALF)], out.at[pl.ds(0, ROWS)]),
        (kp.at[block, pl.ds(0, 16)], out.at[pl.ds(ROWS, 16), pl.ds(0, KCOLS)]),
        (kp.at[block, pl.ds(16, 16)], out.at[pl.ds(ROWS, 16), pl.ds(KCOLS, KCOLS)]),
    ]


def rows_of(kind):
    return PROWS if kind == "P" else ROWS


def load_kernel(groups, n_late, ep, kp, *refs):
    refs = refs[n_late:]
    n = len(groups)
    casts, keeps, buffers, sems = refs[:n], refs[n : 2 * n], refs[2 * n : 3 * n], refs[3 * n]
    dp_index = lax.axis_index("dp")
    x, y, c = dp_index // 8, dp_index // 2 % 4, dp_index % 2
    used = 0
    waits = []
    for group, buffer in zip(groups, buffers):
        for place, piece in enumerate(group):
            block = owner(piece, x, y, 1 - c)
            copies = []
            for source, target in parts_of(piece, block, ep, kp, buffer.at[place]):
                copies.append(pltpu.make_async_copy(source, target, sems.at[used]))
                used += 1
            for copy in copies:
                copy.start()
            waits.append(copies)
    kept = []
    for group, keep in zip(groups, keeps):
        for place, piece in enumerate(group):
            block = owner(piece, x, y, c)
            for source, target in parts_of(piece, block, ep, kp, keep.at[place]):
                copy = pltpu.make_async_copy(source, target, sems.at[used])
                used += 1
                copy.start()
                kept.append(copy)
    at = 0
    for group, buffer, cast in zip(groups, buffers, casts):
        for place, piece in enumerate(group):
            for copy in waits[at]:
                copy.wait()
            at += 1

            def rows(step, carry):
                some = pl.ds(pl.multiple_of(step * 16, 16), 16)
                cast[place, some] = buffer[place, some].astype(BF)
                return carry

            lax.fori_loop(0, rows_of(piece[0]) // 16, rows, 0)
    for copy in kept:
        copy.wait()


def load(ep, kp, groups, late=()):
    shapes = [(len(group), rows_of(group[0][0]), HALF) for group in groups]
    n_copies = 2 * sum(3 if piece[0] == "P" else 1 for group in groups for piece in group)
    vmem = pl.BlockSpec(memory_space=pltpu.VMEM)
    hbm = pl.BlockSpec(memory_space=pltpu.HBM)
    anywhere = pl.BlockSpec(memory_space=pl.ANY)
    out = pl.pallas_call(
        functools.partial(load_kernel, groups, len(late)),
        out_shape=[pltpu.VMEM(shape, BF) for shape in shapes]
        + [pltpu.VMEM(shape, F32) for shape in shapes],
        in_specs=[hbm, hbm] + [anywhere] * len(late),
        out_specs=[vmem] * (2 * len(shapes)),
        scratch_shapes=[pltpu.VMEM(shape, F32) for shape in shapes]
        + [pltpu.SemaphoreType.DMA((n_copies,))],
        compiler_params=pltpu.CompilerParams(vmem_limit_bytes=VMEM_BYTES),
        cost_estimate=pl.CostEstimate(flops=1000, bytes_accessed=1000, transcendentals=0),
    )(ep, kp, *late)
    return out[: len(shapes)], out[len(shapes) :]


def plus(*values):
    total = values[0].astype(F32)
    for value in values[1:]:
        total = total + value.astype(F32)
    return total


def update_kernel(first, second, param, moment, variance, scales, new_param, new_moment, new_variance, grid):
    for j in range(8):
        for h in range(2):
            k = 2 * j + h
            columns = pl.ds(k * BLOCK, BLOCK)
            source = first if k < 8 else second
            grad = source[:ROWS, pl.ds(k % 8 * BLOCK, BLOCK)]
            p, m, v = adam_update(param[0, :, columns], moment[0, :, columns], variance[0, :, columns], grad)
            new_param[0, :, columns] = p
            new_moment[0, :, columns] = m
            new_variance[0, :, columns] = v
            grid[j, :, pl.ds(h * BLOCK, BLOCK)] = to_grid(p, scales[:, k : k + 1])


def update(first, second, param, moment, variance, scales):
    vmem = pl.BlockSpec(memory_space=pltpu.VMEM)
    near = lambda v: pltpu.with_memory_space_constraint(v, pltpu.VMEM)
    return pl.pallas_call(
        update_kernel,
        out_shape=[pltpu.VMEM(param.shape, F32)] * 3 + [pltpu.VMEM((8, ROWS, 256), BF)],
        in_specs=[vmem] * 6,
        out_specs=[vmem] * 4,
        compiler_params=pltpu.CompilerParams(vmem_limit_bytes=VMEM_BYTES),
        cost_estimate=pl.CostEstimate(flops=1000, bytes_accessed=1000, transcendentals=0),
    )(near(first), near(second), near(param), near(moment), near(variance), scales)


def on_device(
    expert_partials,
    key_partials,
    expert_param,
    expert_moment,
    expert_second,
    key_param,
    key_moment,
    key_second,
    expert_scales,
    key_scales,
    rotary_order,
    expert_slot,
):
    dp_index = lax.axis_index("dp")
    expert_index = lax.axis_index("expert")
    x, y, c = dp_index // 8, dp_index // 2 % 4, dp_index % 2
    ep = pltpu.with_memory_space_constraint(expert_partials.reshape(16, ROWS, 2 * HALF), pltpu.HBM)
    kp = pltpu.with_memory_space_constraint(key_partials.reshape(16, KROWS, KCOLS), pltpu.HBM)

    q1_groups = [[("Q", 1, "far")], [("Q", 1, "plain"), ("Q", 1, "near"), ("Q", 1, "own")]]
    far_groups = [[("P", 0, "far"), ("P", 1, "far")]]
    plain_groups = [
        [("P", 0, "plain"), ("P", 1, "plain")],
        [("P", 0, "near"), ("P", 1, "near")],
    ]
    own_groups = [
        [("Q", 0, "far"), ("Q", 0, "plain"), ("Q", 0, "near"), ("Q", 0, "own")],
        [("P", 0, "own"), ("P", 1, "own")],
    ]

    casts_1, keeps_1 = load(ep, kp, q1_groups)
    got_1 = [send(v, 0, 0, 1) for v in casts_1]
    casts_2, keeps_2 = load(ep, kp, far_groups, late=(casts_1[0],))
    got_2 = [send(v, 0, 0, 1) for v in casts_2]
    q1_far = plus(keeps_1[0], got_1[0]).astype(BF)
    x_far = send(q1_far, 1, 0, 0)
    p_far = plus(keeps_2[0], got_2[0]).astype(BF)
    ring_far = ring(p_far)
    q1_rest = plus(keeps_1[1], got_1[1]).astype(BF)
    x_rest = send(q1_rest, 1, 0, 0)
    casts_3, keeps_3 = load(ep, kp, plain_groups, late=(p_far,))
    got_3 = [send(v, 0, 0, 1) for v in casts_3]
    casts_4, keeps_4 = load(ep, kp, own_groups, late=(casts_3[0], q1_rest))
    got_4 = [send(v, 0, 0, 1) for v in casts_4]
    ring_plain = ring(plus(keeps_3[0], got_3[0]).astype(BF))
    ring_near = ring(plus(keeps_3[1], got_3[1], ring_far).astype(BF))
    stay = keeps_4[0], got_4[0]
    ring_q_far = ring(plus(stay[0][:1], stay[1][:1], x_far).astype(BF))
    cross_plain = send(ring_plain, 0, 0, 1)
    p_own = plus(keeps_4[1], got_4[1])
    ring_q_plain = ring(plus(stay[0][1:2], stay[1][1:2], x_rest[0:1]).astype(BF))
    ring_q_near = ring(plus(stay[0][2:3], stay[1][2:3], x_rest[1:2], ring_q_far).astype(BF))
    x_last = send(plus(p_own[1:], ring_near[1:], cross_plain[1:]).astype(BF), 1, 0, 0)
    cross_q_plain = send(ring_q_plain, 0, 0, 1)
    first = plus(p_own[:1], ring_near[:1], cross_plain[:1], x_last)[0]
    second = plus(stay[0][3:], stay[1][3:], x_rest[2:3], cross_q_plain, ring_q_near)[0]

    low = dp_index * ROWS // BLOCK
    my_scales = lax.dynamic_slice(expert_scales, (expert_index, low, 0), (1, 1, 16))[0]
    next_scales = lax.dynamic_slice(
        expert_scales, (expert_index, jnp.minimum(low + 1, 11), 0), (1, 1, 16)
    )[0]
    row_blocks = (dp_index * ROWS + jnp.arange(ROWS, dtype=jnp.int32)) // BLOCK
    row_scales = jnp.where((row_blocks == low)[:, None], my_scales, next_scales)
    new_ep, new_em, new_es, blocks = update(
        first, second, expert_param, expert_moment, expert_second, row_scales
    )
    arrived = lax.all_to_all(blocks, "expert", split_axis=0, concat_axis=0, tiled=True)
    placed = jnp.zeros_like(arrived).at[expert_slot].set(arrived)
    server_expert = jnp.transpose(placed, (0, 2, 1))

    key_grad = jnp.concatenate([first[ROWS:, :KCOLS], first[ROWS:, KCOLS:]], axis=0)
    new_kp, new_km, new_ks = adam_update(key_param, key_moment, key_second, key_grad)
    key_row = lax.dynamic_slice_in_dim(key_scales, dp_index // 4, 1, 0)
    key_grid = to_grid(new_kp, jnp.repeat(key_row, BLOCK, axis=1))
    chip_x = send(key_grid, 1, 0, 0)
    column = jnp.stack([key_grid, chip_x])
    all_y = jnp.stack([column, send(column, 0, -1, 0), send(column, 0, -2, 0), send(column, 0, -3, 0)])
    everything = jnp.stack([all_y, send(all_y, 0, 0, 1)]).reshape(16 * KROWS, KCOLS)
    order = jnp.arange(16 * KROWS, dtype=jnp.int32)
    piece, row = order // KROWS, order % KROWS
    held = dp_of(x + piece % 2, y + piece // 2 % 4, c + piece // 8) * KROWS + row
    head = jnp.arange(HD, dtype=jnp.int32)
    goes = jnp.sum(jnp.where(rotary_order[:, None] == head[None, :], head[:, None], 0), axis=0)
    target = held // HD * HD + jnp.sum(
        jnp.where((held % HD)[:, None] == head[None, :], goes[None, :], 0), axis=1
    )
    pick = (target[:, None] == order[None, :]).astype(BF)
    server_key = lax.dot_general(
        everything, pick, (((0,), (0,)), ((), ())), preferred_element_type=F32
    ).astype(BF)
    return (new_ep, new_em, new_es, new_kp, new_km, new_ks, server_expert, server_key)


def solution(mesh):
    return jax.shard_map(
        on_device,
        mesh=mesh,
        in_specs=(
            P("dp", "expert", None, None),
            P("dp", None, "expert"),
            P("expert", "dp", None),
            P("expert", "dp", None),
            P("expert", "dp", None),
            P("dp", "expert"),
            P("dp", "expert"),
            P("dp", "expert"),
            P(),
            P(None, "expert"),
            P(),
            P(),
        ),
        out_specs=(
            P("expert", "dp", None),
            P("expert", "dp", None),
            P("expert", "dp", None),
            P("dp", "expert"),
            P("dp", "expert"),
            P("dp", "expert"),
            P(None, "expert", "dp"),
            P("expert", None),
        ),
        check_vma=False,
    )
```

```python
import functools

import jax
import jax.numpy as jnp
from jax import lax
from jax.experimental import pallas as pl
from jax.experimental.pallas import tpu as pltpu
from jax.sharding import PartitionSpec as P

HD = 128
BLOCK = 128

BETA_ONE = 0.9
BETA_TWO = 0.95
LEARN = 0.01
DECAY = 0.1
EPSILON = 1e-08
LIMIT = 448.0
CORRECT_ONE = 1.0 - 0.9**10
CORRECT_TWO = 1.0 - 0.95**10

ROWS = 96
KROWS = 32
HALF = 1024
KCOLS = 512
FOLD = 2 * ROWS
KFOLD = 16

BF = jnp.bfloat16
F32 = jnp.float32
VMEM_BYTES = 7 * 1024 * 1024
SLOTS = 6


def dp_of(x, y, c):
    return ((x % 2) * 4 + (y % 4)) * 2 + c % 2


def dp_perm(dx, dy, dc):
    return [
        (dp_of(x, y, c), dp_of(x + dx, y + dy, c + dc))
        for x in range(2)
        for y in range(4)
        for c in range(2)
    ]


def send(value, dx, dy, dc):
    return lax.ppermute(value, "dp", dp_perm(dx, dy, dc))


def ring(value):
    pairs = [
        (dp_of(x, y, c), dp_of(x, y + 1 - 2 * c, c))
        for x in range(2)
        for y in range(4)
        for c in range(2)
    ]
    return lax.ppermute(value, "dp", pairs)


def after(value, *earlier):
    return lax.optimization_barrier((value, *earlier))[0]


def adam_update(param, moment, second, grad):
    moment = BETA_ONE * moment + (1.0 - BETA_ONE) * grad
    second = BETA_TWO * second + (1.0 - BETA_TWO) * grad * grad
    corrected = moment / CORRECT_ONE / (jnp.sqrt(second / CORRECT_TWO) + EPSILON)
    return (param * (1.0 - LEARN * DECAY) - LEARN * corrected, moment, second)


def to_grid(weights, scales):
    return jnp.clip(weights / scales, -LIMIT, LIMIT).astype(BF)


def owner(role, dx, x, y, c):
    step = {"far": 2, "near": 1 - 2 * c, "plain": 1 - 2 * c, "own": 0}[role]
    return dp_of(x + dx, y + 4 + step, 1 - c if role == "plain" else c)


def parts_of(batch, role, x, y, c, ep, kp, out):
    block = owner(role, 1 if batch == "turn" else 0, x, y, c)
    parts = [
        (ep.at[block, :, pl.ds(half * HALF, HALF)], out.at[pl.ds(half * ROWS, ROWS)])
        for half in range(2)
    ]
    if batch == "turn":
        for place, dx in enumerate((1, 0)):
            block = owner(role, dx, x, y, c)
            target = out.at[pl.ds(FOLD + place * KFOLD, KFOLD)]
            parts += [
                (kp.at[block, pl.ds(part * KFOLD, KFOLD)], target.at[:, pl.ds(part * KCOLS, KCOLS)])
                for part in range(2)
            ]
    return parts


def rows_of(batch):
    return FOLD + 2 * KFOLD if batch == "turn" else FOLD


def load_kernel(batch, roles, n_late, ep, kp, *refs):
    refs = refs[n_late:]
    n = len(roles)
    casts, keeps, buffer, sems = refs[:n], refs[n : 2 * n], refs[2 * n], refs[2 * n + 1]
    dp_index = lax.axis_index("dp")
    x, y, c = dp_index // 8, dp_index // 2 % 4, dp_index % 2
    work = [(role, 1 - c, out) for role, out in zip(roles, casts)]
    work += [(role, c, out) for role, out in zip(roles, keeps)]

    def start(index):
        role, core, _ = work[index]
        slot = index % SLOTS
        copies = [
            pltpu.make_async_copy(source, target, sems.at[slot, number])
            for number, (source, target) in enumerate(
                parts_of(batch, role, x, y, core, ep, kp, buffer.at[slot])
            )
        ]
        for copy in copies:
            copy.start()
        return copies

    flying = [start(index) for index in range(min(SLOTS, len(work)))]
    for index, (_, _, out) in enumerate(work):
        for copy in flying[index]:
            copy.wait()
        slot = index % SLOTS

        def rows(step, carry):
            some = pl.ds(pl.multiple_of(step * 16, 16), 16)
            out[0, some] = buffer[slot, some].astype(BF)
            return carry

        lax.fori_loop(0, rows_of(batch) // 16, rows, 0)
        if index + SLOTS < len(work):
            flying.append(start(index + SLOTS))


def load(ep, kp, batch, roles, late=()):
    shape = (1, rows_of(batch), HALF)
    vmem = pl.BlockSpec(memory_space=pltpu.VMEM)
    hbm = pl.BlockSpec(memory_space=pltpu.HBM)
    anywhere = pl.BlockSpec(memory_space=pl.ANY)
    out = pl.pallas_call(
        functools.partial(load_kernel, batch, roles, len(late)),
        out_shape=[jax.ShapeDtypeStruct(shape, BF)] * (2 * len(roles)),
        in_specs=[hbm, hbm] + [anywhere] * len(late),
        out_specs=[vmem] * (2 * len(roles)),
        scratch_shapes=[
            pltpu.VMEM((SLOTS,) + shape[1:], F32),
            pltpu.SemaphoreType.DMA((SLOTS, 6)),
        ],
        compiler_params=pltpu.CompilerParams(vmem_limit_bytes=VMEM_BYTES),
        cost_estimate=pl.CostEstimate(flops=1000, bytes_accessed=1000, transcendentals=0),
    )(ep, kp, *late)
    return out[: len(roles)], out[len(roles) :]


def plus(*values):
    total = values[0].astype(F32)
    for value in values[1:]:
        total = total + value.astype(F32)
    return total


def update_kernel(*refs):
    terms, (param, moment, variance, scales), results, grid = refs[:4], refs[4:8], refs[8:11], refs[11]
    start = lax.axis_index("dp") * ROWS
    low = start // BLOCK
    expert = lax.axis_index("expert")
    row = lax.broadcasted_iota(jnp.int32, (ROWS, 16), 0) + start
    row_scales = jnp.where(
        row < (low + 1) * BLOCK,
        scales[expert, pl.ds(low, 1), :],
        scales[expert, pl.ds(jnp.minimum(low + 1, 11), 1), :],
    )
    for j in range(8):
        for h in range(2):
            k = 2 * j + h
            columns = pl.ds(k * BLOCK, BLOCK)
            held = pl.ds(k % 8 * BLOCK, BLOCK)
            rows = pl.ds(k // 8 * ROWS, ROWS)
            grad = terms[0][0, rows, held].astype(F32)
            for term in terms[1:]:
                grad = grad + term[0, rows, held].astype(F32)
            new = adam_update(param[0, :, columns], moment[0, :, columns], variance[0, :, columns], grad)
            for result, value in zip(results, new):
                result[0, :, columns] = value
            grid[j, :, pl.ds(h * BLOCK, BLOCK)] = to_grid(new[0], row_scales[:, k : k + 1])


def key_kernel(own, arrived, param, moment, variance, scales, *results):
    quarter = lax.axis_index("dp") * KROWS // BLOCK
    row_scales = scales[pl.ds(quarter, 1), :]
    for part in range(2):
        rows = pl.ds(part * KFOLD, KFOLD)
        for k in range(KCOLS // BLOCK):
            columns = pl.ds(k * BLOCK, BLOCK)
            held = pl.ds(part * KCOLS + k * BLOCK, BLOCK)
            grad = own[0, FOLD + KFOLD :, held] + arrived[0, FOLD:, held].astype(F32)
            new = adam_update(param[rows, columns], moment[rows, columns], variance[rows, columns], grad)
            for result, value in zip(results, new):
                result[rows, columns] = value
            results[3][rows, columns] = to_grid(new[0], row_scales[:, k : k + 1])


def update(kernel, terms, param, moment, variance, scales, grid_shape):
    vmem = pl.BlockSpec(memory_space=pltpu.VMEM)
    near = lambda v: pltpu.with_memory_space_constraint(v, pltpu.VMEM)
    return pl.pallas_call(
        kernel,
        out_shape=[pltpu.VMEM(param.shape, F32)] * 3 + [jax.ShapeDtypeStruct(grid_shape, BF)],
        in_specs=[vmem] * (len(terms) + 4),
        out_specs=[vmem] * 4,
        compiler_params=pltpu.CompilerParams(vmem_limit_bytes=VMEM_BYTES),
        cost_estimate=pl.CostEstimate(flops=1000, bytes_accessed=1000, transcendentals=0),
    )(*terms, near(param), near(moment), near(variance), scales)


def on_device(
    expert_partials,
    key_partials,
    expert_param,
    expert_moment,
    expert_second,
    key_param,
    key_moment,
    key_second,
    expert_scales,
    key_scales,
    rotary_order,
    expert_slot,
):
    dp_index = lax.axis_index("dp")
    x, y, c = dp_index // 8, dp_index // 2 % 4, dp_index % 2
    expert_partials, x, y, c = lax.optimization_barrier((expert_partials, x, y, c))
    ep = pltpu.with_memory_space_constraint(expert_partials.reshape(16, ROWS, 2 * HALF), pltpu.HBM)
    kp = pltpu.with_memory_space_constraint(key_partials.reshape(16, KROWS, KCOLS), pltpu.HBM)

    across = lambda values: [send(value, 0, 0, 1) for value in values]
    casts, keeps = load(ep, kp, "turn", ["far", "plain"])
    got = across(casts)
    casts_b, keeps_b = load(ep, kp, "turn", ["near", "own"], late=(casts[0],))
    got_b = across(casts_b)
    casts_c, keeps_c = load(ep, kp, "stay", ["far", "plain", "near", "own"], late=(casts_b[0],))
    got_c = across(casts_c)
    far = ring(plus(keeps[0], got[0]).astype(BF))
    plain = ring(plus(keeps[1], got[1]).astype(BF))
    near = ring(plus(keeps_b[0], got_b[0], far).astype(BF))
    cross = send(plain, 0, 0, 1)
    far_c = ring(plus(keeps_c[0], got_c[0]).astype(BF))
    plain_c = ring(plus(keeps_c[1], got_c[1]).astype(BF))
    turned = plus(keeps_b[1], got_b[1], cross, near)
    x_last = send(turned[:, : FOLD + KFOLD].astype(BF), 1, 0, 0)
    near_c = ring(plus(keeps_c[2], got_c[2], far_c).astype(BF))
    cross_c = send(plain_c, 0, 0, 1)
    stayed = plus(keeps_c[3], got_c[3]).astype(BF)
    new_ep, new_em, new_es, blocks = update(
        update_kernel,
        (stayed, cross_c, near_c, x_last),
        expert_param,
        expert_moment,
        expert_second,
        expert_scales,
        (8, ROWS, 256),
    )
    arrived = lax.all_to_all(blocks, "expert", split_axis=0, concat_axis=0, tiled=True)
    placed = jnp.zeros_like(arrived).at[expert_slot].set(arrived)
    server_expert = jnp.transpose(placed, (0, 2, 1))

    new_kp, new_km, new_ks, key_grid = update(
        key_kernel,
        (turned, x_last),
        key_param,
        key_moment,
        key_second,
        key_scales,
        (KROWS, KCOLS),
    )
    chip_x = send(after(key_grid, far_c), 1, 0, 0)
    column = after(jnp.stack([key_grid, chip_x]), near_c)
    all_y = jnp.stack([column, send(column, 0, -1, 0), send(column, 0, -2, 0), send(column, 0, -3, 0)])
    everything = jnp.stack([all_y, send(all_y, 0, 0, 1)]).reshape(16 * KROWS, KCOLS)
    order = jnp.arange(16 * KROWS, dtype=jnp.int32)
    piece, row = order // KROWS, order % KROWS
    held = dp_of(x + piece % 2, y + piece // 2 % 4, c + piece // 8) * KROWS + row
    head = jnp.arange(HD, dtype=jnp.int32)
    goes = jnp.sum(jnp.where(rotary_order[:, None] == head[None, :], head[:, None], 0), axis=0)
    target = held // HD * HD + jnp.sum(
        jnp.where((held % HD)[:, None] == head[None, :], goes[None, :], 0), axis=1
    )
    pick = (target[:, None] == order[None, :]).astype(BF)
    server_key = lax.dot_general(
        everything, pick, (((0,), (0,)), ((), ())), preferred_element_type=F32
    ).astype(BF)
    return (new_ep, new_em, new_es, new_kp, new_km, new_ks, server_expert, server_key)


def solution(mesh):
    return jax.shard_map(
        on_device,
        mesh=mesh,
        in_specs=(
            P("dp", "expert", None, None),
            P("dp", None, "expert"),
            P("expert", "dp", None),
            P("expert", "dp", None),
            P("expert", "dp", None),
            P("dp", "expert"),
            P("dp", "expert"),
            P("dp", "expert"),
            P(),
            P(None, "expert"),
            P(),
            P(),
        ),
        out_specs=(
            P("expert", "dp", None),
            P("expert", "dp", None),
            P("expert", "dp", None),
            P("dp", "expert"),
            P("dp", "expert"),
            P("dp", "expert"),
            P(None, "expert", "dp"),
            P("expert", None),
        ),
        check_vma=False,
    )
```

```python
import functools

import jax
import jax.numpy as jnp
from jax import lax
from jax.experimental import pallas as pl
from jax.experimental.pallas import tpu as pltpu
from jax.sharding import PartitionSpec as P

HD = 128
BLOCK = 128

BETA_ONE = 0.9
BETA_TWO = 0.95
LEARN = 0.01
DECAY = 0.1
EPSILON = 1e-08
LIMIT = 448.0
CORRECT_ONE = 1.0 - 0.9**10
CORRECT_TWO = 1.0 - 0.95**10

ROWS = 96
KROWS = 32
HALF = 1024
KCOLS = 512
FOLD = 2 * ROWS
KFOLD = 16

BF = jnp.bfloat16
F32 = jnp.float32
VMEM_BYTES = 7 * 1024 * 1024
SLOTS = 6


def dp_of(x, y, c):
    return ((x % 2) * 4 + (y % 4)) * 2 + c % 2


def dp_perm(dx, dy, dc):
    return [
        (dp_of(x, y, c), dp_of(x + dx, y + dy, c + dc))
        for x in range(2)
        for y in range(4)
        for c in range(2)
    ]


def send(value, dx, dy, dc):
    return lax.ppermute(value, "dp", dp_perm(dx, dy, dc))


def ring(value):
    pairs = [
        (dp_of(x, y, c), dp_of(x, y + 1 - 2 * c, c))
        for x in range(2)
        for y in range(4)
        for c in range(2)
    ]
    return lax.ppermute(value, "dp", pairs)


def adam_update(param, moment, second, grad):
    moment = BETA_ONE * moment + (1.0 - BETA_ONE) * grad
    second = BETA_TWO * second + (1.0 - BETA_TWO) * grad * grad
    corrected = moment / CORRECT_ONE / (jnp.sqrt(second / CORRECT_TWO) + EPSILON)
    return (param * (1.0 - LEARN * DECAY) - LEARN * corrected, moment, second)


def to_grid(weights, scales):
    return jnp.clip(weights / scales, -LIMIT, LIMIT).astype(BF)


def owner(role, dx, x, y, c):
    step = {"far": 2, "near": 1 - 2 * c, "plain": 1 - 2 * c, "own": 0}[role]
    return dp_of(x + dx, y + 4 + step, 1 - c if role == "plain" else c)


def parts_of(batch, role, x, y, c, ep, kp, out):
    block = owner(role, 1 if batch == "turn" else 0, x, y, c)
    parts = [
        (ep.at[block, :, pl.ds(half * HALF, HALF)], out.at[pl.ds(half * ROWS, ROWS)])
        for half in range(2)
    ]
    if batch == "turn":
        for place, dx in enumerate((1, 0)):
            block = owner(role, dx, x, y, c)
            target = out.at[pl.ds(FOLD + place * KFOLD, KFOLD)]
            parts += [
                (kp.at[block, pl.ds(part * KFOLD, KFOLD)], target.at[:, pl.ds(part * KCOLS, KCOLS)])
                for part in range(2)
            ]
    return parts


def rows_of(batch):
    return FOLD + 2 * KFOLD if batch == "turn" else FOLD


def load_kernel(batch, roles, n_late, ep, kp, *refs):
    refs = refs[n_late:]
    n = len(roles)
    casts, keeps, buffer, sems = refs[:n], refs[n : 2 * n], refs[2 * n], refs[2 * n + 1]
    dp_index = lax.axis_index("dp")
    x, y, c = dp_index // 8, dp_index // 2 % 4, dp_index % 2
    work = [(role, 1 - c, out) for role, out in zip(roles, casts)]
    work += [(role, c, out) for role, out in zip(roles, keeps)]

    def start(index):
        role, core, _ = work[index]
        slot = index % SLOTS
        copies = [
            pltpu.make_async_copy(source, target, sems.at[slot, number])
            for number, (source, target) in enumerate(
                parts_of(batch, role, x, y, core, ep, kp, buffer.at[slot])
            )
        ]
        for copy in copies:
            copy.start()
        return copies

    flying = [start(index) for index in range(min(SLOTS, len(work)))]
    for index, (_, _, out) in enumerate(work):
        for copy in flying[index]:
            copy.wait()
        slot = index % SLOTS

        def rows(step, carry):
            some = pl.ds(pl.multiple_of(step * 16, 16), 16)
            out[0, some] = buffer[slot, some].astype(BF)
            return carry

        lax.fori_loop(0, rows_of(batch) // 16, rows, 0)
        if index + SLOTS < len(work):
            flying.append(start(index + SLOTS))


def load(ep, kp, batch, roles, late=()):
    shape = (1, rows_of(batch), HALF)
    vmem = pl.BlockSpec(memory_space=pltpu.VMEM)
    hbm = pl.BlockSpec(memory_space=pltpu.HBM)
    anywhere = pl.BlockSpec(memory_space=pl.ANY)
    out = pl.pallas_call(
        functools.partial(load_kernel, batch, roles, len(late)),
        out_shape=[jax.ShapeDtypeStruct(shape, BF)] * (2 * len(roles)),
        in_specs=[hbm, hbm] + [anywhere] * len(late),
        out_specs=[vmem] * (2 * len(roles)),
        scratch_shapes=[
            pltpu.VMEM((SLOTS,) + shape[1:], F32),
            pltpu.SemaphoreType.DMA((SLOTS, 6)),
        ],
        compiler_params=pltpu.CompilerParams(vmem_limit_bytes=VMEM_BYTES),
        cost_estimate=pl.CostEstimate(flops=1000, bytes_accessed=1000, transcendentals=0),
    )(ep, kp, *late)
    return out[: len(roles)], out[len(roles) :]


def plus(*values):
    total = values[0].astype(F32)
    for value in values[1:]:
        total = total + value.astype(F32)
    return total


def update_kernel(*refs):
    terms, (param, moment, variance, scales), results, grid = refs[:4], refs[4:8], refs[8:11], refs[11]
    start = lax.axis_index("dp") * ROWS
    low = start // BLOCK
    expert = lax.axis_index("expert")
    row = lax.broadcasted_iota(jnp.int32, (ROWS, 16), 0) + start
    row_scales = jnp.where(
        row < (low + 1) * BLOCK,
        scales[expert, pl.ds(low, 1), :],
        scales[expert, pl.ds(jnp.minimum(low + 1, 11), 1), :],
    )
    for j in range(8):
        for h in range(2):
            k = 2 * j + h
            columns = pl.ds(k * BLOCK, BLOCK)
            held = pl.ds(k % 8 * BLOCK, BLOCK)
            rows = pl.ds(k // 8 * ROWS, ROWS)
            grad = terms[0][0, rows, held].astype(F32)
            for term in terms[1:]:
                grad = grad + term[0, rows, held].astype(F32)
            new = adam_update(param[0, :, columns], moment[0, :, columns], variance[0, :, columns], grad)
            for result, value in zip(results, new):
                result[0, :, columns] = value
            grid[j, :, pl.ds(h * BLOCK, BLOCK)] = to_grid(new[0], row_scales[:, k : k + 1])


def key_kernel(own, arrived, param, moment, variance, scales, *results):
    quarter = lax.axis_index("dp") * KROWS // BLOCK
    row_scales = scales[pl.ds(quarter, 1), :]
    for part in range(2):
        rows = pl.ds(part * KFOLD, KFOLD)
        for k in range(KCOLS // BLOCK):
            columns = pl.ds(k * BLOCK, BLOCK)
            held = pl.ds(part * KCOLS + k * BLOCK, BLOCK)
            grad = own[0, FOLD + KFOLD :, held] + arrived[0, FOLD:, held].astype(F32)
            new = adam_update(param[rows, columns], moment[rows, columns], variance[rows, columns], grad)
            for result, value in zip(results, new):
                result[rows, columns] = value
            results[3][rows, columns] = to_grid(new[0], row_scales[:, k : k + 1])


def update(kernel, terms, param, moment, variance, scales, grid_shape):
    vmem = pl.BlockSpec(memory_space=pltpu.VMEM)
    near = lambda v: pltpu.with_memory_space_constraint(v, pltpu.VMEM)
    return pl.pallas_call(
        kernel,
        out_shape=[jax.ShapeDtypeStruct(param.shape, F32)] * 3 + [jax.ShapeDtypeStruct(grid_shape, BF)],
        in_specs=[vmem] * (len(terms) + 4),
        out_specs=[vmem] * 4,
        compiler_params=pltpu.CompilerParams(vmem_limit_bytes=VMEM_BYTES),
        cost_estimate=pl.CostEstimate(flops=1000, bytes_accessed=1000, transcendentals=0),
    )(*terms, near(param), near(moment), near(variance), scales)


def on_device(
    expert_partials,
    key_partials,
    expert_param,
    expert_moment,
    expert_second,
    key_param,
    key_moment,
    key_second,
    expert_scales,
    key_scales,
    rotary_order,
    expert_slot,
):
    dp_index = lax.axis_index("dp")
    x, y, c = dp_index // 8, dp_index // 2 % 4, dp_index % 2
    expert_partials, x, y, c = lax.optimization_barrier((expert_partials, x, y, c))
    ep = pltpu.with_memory_space_constraint(expert_partials.reshape(16, ROWS, 2 * HALF), pltpu.HBM)
    kp = pltpu.with_memory_space_constraint(key_partials.reshape(16, KROWS, KCOLS), pltpu.HBM)

    across = lambda values: [send(value, 0, 0, 1) for value in values]
    casts, keeps = load(ep, kp, "turn", ["far", "plain"])
    got = across(casts)
    casts_b, keeps_b = load(ep, kp, "turn", ["near", "own"], late=(casts[0],))
    got_b = across(casts_b)
    casts_c, keeps_c = load(ep, kp, "stay", ["far", "plain", "near", "own"], late=(casts_b[0],))
    got_c = across(casts_c)
    far = ring(plus(keeps[0], got[0]).astype(BF))
    plain = ring(plus(keeps[1], got[1]).astype(BF))
    near = ring(plus(keeps_b[0], got_b[0], far).astype(BF))
    cross = send(plain, 0, 0, 1)
    far_c = ring(plus(keeps_c[0], got_c[0]).astype(BF))
    plain_c = ring(plus(keeps_c[1], got_c[1]).astype(BF))
    turned = plus(keeps_b[1], got_b[1], cross, near)
    x_last = send(turned[:, : FOLD + KFOLD].astype(BF), 1, 0, 0)
    near_c = ring(plus(keeps_c[2], got_c[2], far_c).astype(BF))
    cross_c = send(plain_c, 0, 0, 1)
    stayed = plus(keeps_c[3], got_c[3]).astype(BF)
    new_kp, new_km, new_ks, key_grid = update(
        key_kernel,
        (turned, x_last),
        key_param,
        key_moment,
        key_second,
        key_scales,
        (KROWS, KCOLS),
    )
    chip_x = send(key_grid, 1, 0, 0)
    new_ep, new_em, new_es, blocks = update(
        update_kernel,
        (stayed, cross_c, near_c, x_last),
        expert_param,
        expert_moment,
        expert_second,
        expert_scales,
        (8, ROWS, 256),
    )
    column = jnp.stack([key_grid, chip_x])
    column, blocks = lax.optimization_barrier((column, blocks))
    arrived = lax.all_to_all(blocks, "expert", split_axis=0, concat_axis=0, tiled=True)
    all_y = [column] + [send(column, 0, -step, 0) for step in (1, 2, 3)]
    all_y, arrived = lax.optimization_barrier((all_y, arrived))
    all_y = jnp.stack(all_y)
    everything = jnp.stack([all_y, send(all_y, 0, 0, 1)]).reshape(16 * KROWS, KCOLS)
    order = jnp.arange(16 * KROWS, dtype=jnp.int32)
    piece, row = order // KROWS, order % KROWS
    held = dp_of(x + piece % 2, y + piece // 2 % 4, c + piece // 8) * KROWS + row
    head = jnp.arange(HD, dtype=jnp.int32)
    goes = jnp.sum(jnp.where(rotary_order[:, None] == head[None, :], head[:, None], 0), axis=0)
    target = held // HD * HD + jnp.sum(
        jnp.where((held % HD)[:, None] == head[None, :], goes[None, :], 0), axis=1
    )
    pick = (target[:, None] == order[None, :]).astype(BF)
    server_key = lax.dot_general(
        everything, pick, (((0,), (0,)), ((), ())), preferred_element_type=F32
    ).astype(BF)
    placed = jnp.zeros_like(arrived).at[expert_slot].set(arrived)
    server_expert = jnp.transpose(placed, (0, 2, 1))
    return (new_ep, new_em, new_es, new_kp, new_km, new_ks, server_expert, server_key)


def solution(mesh):
    return jax.shard_map(
        on_device,
        mesh=mesh,
        in_specs=(
            P("dp", "expert", None, None),
            P("dp", None, "expert"),
            P("expert", "dp", None),
            P("expert", "dp", None),
            P("expert", "dp", None),
            P("dp", "expert"),
            P("dp", "expert"),
            P("dp", "expert"),
            P(),
            P(None, "expert"),
            P(),
            P(),
        ),
        out_specs=(
            P("expert", "dp", None),
            P("expert", "dp", None),
            P("expert", "dp", None),
            P("dp", "expert"),
            P("dp", "expert"),
            P("dp", "expert"),
            P(None, "expert", "dp"),
            P("expert", None),
        ),
        check_vma=False,
    )
```

```python
import functools

import jax
import jax.numpy as jnp
from jax import lax
from jax.experimental import pallas as pl
from jax.experimental.pallas import tpu as pltpu
from jax.sharding import PartitionSpec as P

HD = 128
BLOCK = 128

BETA_ONE = 0.9
BETA_TWO = 0.95
LEARN = 0.01
DECAY = 0.1
EPSILON = 1e-08
LIMIT = 448.0
CORRECT_ONE = 1.0 - 0.9**10
CORRECT_TWO = 1.0 - 0.95**10

ROWS = 96
KROWS = 32
HALF = 1024
KCOLS = 512
FOLD = 2 * ROWS
KFOLD = 16

BF = jnp.bfloat16
F32 = jnp.float32
VMEM_BYTES = 7 * 1024 * 1024
SLOTS = 6


def dp_of(x, y, c):
    return ((x % 2) * 4 + (y % 4)) * 2 + c % 2


def dp_perm(dx, dy, dc):
    return [
        (dp_of(x, y, c), dp_of(x + dx, y + dy, c + dc))
        for x in range(2)
        for y in range(4)
        for c in range(2)
    ]


def send(value, dx, dy, dc):
    return lax.ppermute(value, "dp", dp_perm(dx, dy, dc))


def ring(value):
    pairs = [
        (dp_of(x, y, c), dp_of(x, y + 1 - 2 * c, c))
        for x in range(2)
        for y in range(4)
        for c in range(2)
    ]
    return lax.ppermute(value, "dp", pairs)


def adam_update(param, moment, second, grad):
    moment = BETA_ONE * moment + (1.0 - BETA_ONE) * grad
    second = BETA_TWO * second + (1.0 - BETA_TWO) * grad * grad
    corrected = moment / CORRECT_ONE / (jnp.sqrt(second / CORRECT_TWO) + EPSILON)
    return (param * (1.0 - LEARN * DECAY) - LEARN * corrected, moment, second)


def to_grid(weights, scales):
    return jnp.clip(weights / scales, -LIMIT, LIMIT).astype(BF)


def owner(role, dx, x, y, c):
    step = {"far": 2, "near": 1 - 2 * c, "plain": 1 - 2 * c, "own": 0}[role]
    return dp_of(x + dx, y + 4 + step, 1 - c if role == "plain" else c)


def parts_of(batch, role, x, y, c, ep, kp, out):
    block = owner(role, 1 if batch == "turn" else 0, x, y, c)
    parts = [
        (ep.at[block, :, pl.ds(half * HALF, HALF)], out.at[pl.ds(half * ROWS, ROWS)])
        for half in range(2)
    ]
    if batch == "turn":
        for place, dx in enumerate((1, 0)):
            block = owner(role, dx, x, y, c)
            target = out.at[pl.ds(FOLD + place * KFOLD, KFOLD)]
            parts += [
                (kp.at[block, pl.ds(part * KFOLD, KFOLD)], target.at[:, pl.ds(part * KCOLS, KCOLS)])
                for part in range(2)
            ]
    return parts


def rows_of(batch):
    return FOLD + 2 * KFOLD if batch == "turn" else FOLD


def load_kernel(batch, roles, n_late, ep, kp, *refs):
    refs = refs[n_late:]
    n = len(roles)
    casts, keeps, buffer, sems = refs[:n], refs[n : 2 * n], refs[2 * n], refs[2 * n + 1]
    dp_index = lax.axis_index("dp")
    x, y, c = dp_index // 8, dp_index // 2 % 4, dp_index % 2
    work = [(role, 1 - c, out) for role, out in zip(roles, casts)]
    work += [(role, c, out) for role, out in zip(roles, keeps)]

    def start(index):
        role, core, _ = work[index]
        slot = index % SLOTS
        copies = [
            pltpu.make_async_copy(source, target, sems.at[slot, number])
            for number, (source, target) in enumerate(
                parts_of(batch, role, x, y, core, ep, kp, buffer.at[slot])
            )
        ]
        for copy in copies:
            copy.start()
        return copies

    flying = [start(index) for index in range(min(SLOTS, len(work)))]
    for index, (_, _, out) in enumerate(work):
        for copy in flying[index]:
            copy.wait()
        slot = index % SLOTS

        def rows(step, carry):
            some = pl.ds(pl.multiple_of(step * 16, 16), 16)
            out[0, some] = buffer[slot, some].astype(BF)
            return carry

        lax.fori_loop(0, rows_of(batch) // 16, rows, 0)
        if index + SLOTS < len(work):
            flying.append(start(index + SLOTS))


def load(ep, kp, batch, roles, late=()):
    shape = (1, rows_of(batch), HALF)
    vmem = pl.BlockSpec(memory_space=pltpu.VMEM)
    hbm = pl.BlockSpec(memory_space=pltpu.HBM)
    anywhere = pl.BlockSpec(memory_space=pl.ANY)
    out = pl.pallas_call(
        functools.partial(load_kernel, batch, roles, len(late)),
        out_shape=[jax.ShapeDtypeStruct(shape, BF)] * (2 * len(roles)),
        in_specs=[hbm, hbm] + [anywhere] * len(late),
        out_specs=[vmem] * (2 * len(roles)),
        scratch_shapes=[
            pltpu.VMEM((SLOTS,) + shape[1:], F32),
            pltpu.SemaphoreType.DMA((SLOTS, 6)),
        ],
        compiler_params=pltpu.CompilerParams(vmem_limit_bytes=VMEM_BYTES),
        cost_estimate=pl.CostEstimate(flops=1000, bytes_accessed=1000, transcendentals=0),
    )(ep, kp, *late)
    return out[: len(roles)], out[len(roles) :]


def plus(*values):
    total = values[0].astype(F32)
    for value in values[1:]:
        total = total + value.astype(F32)
    return total


def update_kernel(*refs):
    terms, (param, moment, variance, scales), results, grid = refs[:5], refs[5:9], refs[9:12], refs[12]
    start = lax.axis_index("dp") * ROWS
    low = start // BLOCK
    expert = lax.axis_index("expert")
    row = lax.broadcasted_iota(jnp.int32, (ROWS, 16), 0) + start
    row_scales = jnp.where(
        row < (low + 1) * BLOCK,
        scales[expert, pl.ds(low, 1), :],
        scales[expert, pl.ds(jnp.minimum(low + 1, 11), 1), :],
    )
    for j in range(8):
        for h in range(2):
            k = 2 * j + h
            columns = pl.ds(k * BLOCK, BLOCK)
            held = pl.ds(k % 8 * BLOCK, BLOCK)
            rows = pl.ds(k // 8 * ROWS, ROWS)
            grad = terms[0][0, rows, held].astype(F32)
            for term in terms[1:3]:
                grad = grad + term[0, rows, held].astype(F32)
            grad = grad + terms[3 + k // 8][0, :ROWS, held].astype(F32)
            new = adam_update(param[0, :, columns], moment[0, :, columns], variance[0, :, columns], grad)
            for result, value in zip(results, new):
                result[0, :, columns] = value
            grid[j, :, pl.ds(h * BLOCK, BLOCK)] = to_grid(new[0], row_scales[:, k : k + 1])


def key_kernel(own, arrived, param, moment, variance, scales, *results):
    quarter = lax.axis_index("dp") * KROWS // BLOCK
    row_scales = scales[pl.ds(quarter, 1), :]
    for part in range(2):
        rows = pl.ds(part * KFOLD, KFOLD)
        for k in range(KCOLS // BLOCK):
            columns = pl.ds(k * BLOCK, BLOCK)
            held = pl.ds(part * KCOLS + k * BLOCK, BLOCK)
            grad = own[0, FOLD + KFOLD :, held] + arrived[0, ROWS:, held].astype(F32)
            new = adam_update(param[rows, columns], moment[rows, columns], variance[rows, columns], grad)
            for result, value in zip(results, new):
                result[rows, columns] = value
            results[3][rows, columns] = to_grid(new[0], row_scales[:, k : k + 1])


def update(kernel, terms, param, moment, variance, scales, grid_shape):
    vmem = pl.BlockSpec(memory_space=pltpu.VMEM)
    near = lambda v: pltpu.with_memory_space_constraint(v, pltpu.VMEM)
    return pl.pallas_call(
        kernel,
        out_shape=[jax.ShapeDtypeStruct(param.shape, F32)] * 3 + [jax.ShapeDtypeStruct(grid_shape, BF)],
        in_specs=[vmem] * (len(terms) + 4),
        out_specs=[vmem] * 4,
        compiler_params=pltpu.CompilerParams(vmem_limit_bytes=VMEM_BYTES),
        cost_estimate=pl.CostEstimate(flops=1000, bytes_accessed=1000, transcendentals=0),
    )(*terms, near(param), near(moment), near(variance), scales)


def on_device(
    expert_partials,
    key_partials,
    expert_param,
    expert_moment,
    expert_second,
    key_param,
    key_moment,
    key_second,
    expert_scales,
    key_scales,
    rotary_order,
    expert_slot,
):
    dp_index = lax.axis_index("dp")
    x, y, c = dp_index // 8, dp_index // 2 % 4, dp_index % 2
    expert_partials, x, y, c = lax.optimization_barrier((expert_partials, x, y, c))
    ep = pltpu.with_memory_space_constraint(expert_partials.reshape(16, ROWS, 2 * HALF), pltpu.HBM)
    kp = pltpu.with_memory_space_constraint(key_partials.reshape(16, KROWS, KCOLS), pltpu.HBM)

    across = lambda values: [send(value, 0, 0, 1) for value in values]
    casts, keeps = load(ep, kp, "turn", ["far", "plain"])
    got = across(casts)
    casts_b, keeps_b = load(ep, kp, "turn", ["near", "own"], late=(casts[0],))
    got_b = across(casts_b)
    casts_c, keeps_c = load(ep, kp, "stay", ["far", "plain", "near", "own"], late=(casts_b[0],))
    got_c = across(casts_c)
    far = ring(plus(keeps[0], got[0]).astype(BF))
    plain = ring(plus(keeps[1], got[1]).astype(BF))
    near = ring(plus(keeps_b[0], got_b[0], far).astype(BF))
    cross = send(plain, 0, 0, 1)
    far_c = ring(plus(keeps_c[0], got_c[0]).astype(BF))
    plain_c = ring(plus(keeps_c[1], got_c[1]).astype(BF))
    turned = plus(keeps_b[1], got_b[1], cross, near)
    x_late = send(turned[:, :ROWS].astype(BF), 1, 0, 0)
    x_last = send(turned[:, ROWS : FOLD + KFOLD].astype(BF), 1, 0, 0)
    near_c = ring(plus(keeps_c[2], got_c[2], far_c).astype(BF))
    cross_c = send(plain_c, 0, 0, 1)
    stayed = plus(keeps_c[3], got_c[3]).astype(BF)
    new_kp, new_km, new_ks, key_grid = update(
        key_kernel,
        (turned, x_last),
        key_param,
        key_moment,
        key_second,
        key_scales,
        (KROWS, KCOLS),
    )
    key_grid, x_late = lax.optimization_barrier((key_grid, x_late))
    chip_x = send(key_grid, 1, 0, 0)
    new_ep, new_em, new_es, blocks = update(
        update_kernel,
        (stayed, cross_c, near_c, x_late, x_last),
        expert_param,
        expert_moment,
        expert_second,
        expert_scales,
        (8, ROWS, 256),
    )
    column = jnp.stack([key_grid, chip_x])
    column, blocks = lax.optimization_barrier((column, blocks))
    arrived = lax.all_to_all(blocks, "expert", split_axis=0, concat_axis=0, tiled=True)
    all_y = [column] + [send(column, 0, -step, 0) for step in (1, 2, 3)]
    all_y, arrived = lax.optimization_barrier((all_y, arrived))
    all_y = jnp.stack(all_y)
    everything = jnp.stack([all_y, send(all_y, 0, 0, 1)]).reshape(16 * KROWS, KCOLS)
    order = jnp.arange(16 * KROWS, dtype=jnp.int32)
    piece, row = order // KROWS, order % KROWS
    held = dp_of(x + piece % 2, y + piece // 2 % 4, c + piece // 8) * KROWS + row
    head = jnp.arange(HD, dtype=jnp.int32)
    goes = jnp.sum(jnp.where(rotary_order[:, None] == head[None, :], head[:, None], 0), axis=0)
    target = held // HD * HD + jnp.sum(
        jnp.where((held % HD)[:, None] == head[None, :], goes[None, :], 0), axis=1
    )
    pick = (target[:, None] == order[None, :]).astype(BF)
    server_key = lax.dot_general(
        everything, pick, (((0,), (0,)), ((), ())), preferred_element_type=F32
    ).astype(BF)
    placed = jnp.zeros_like(arrived).at[expert_slot].set(arrived)
    server_expert = jnp.transpose(placed, (0, 2, 1))
    return (new_ep, new_em, new_es, new_kp, new_km, new_ks, server_expert, server_key)


def solution(mesh):
    return jax.shard_map(
        on_device,
        mesh=mesh,
        in_specs=(
            P("dp", "expert", None, None),
            P("dp", None, "expert"),
            P("expert", "dp", None),
            P("expert", "dp", None),
            P("expert", "dp", None),
            P("dp", "expert"),
            P("dp", "expert"),
            P("dp", "expert"),
            P(),
            P(None, "expert"),
            P(),
            P(),
        ),
        out_specs=(
            P("expert", "dp", None),
            P("expert", "dp", None),
            P("expert", "dp", None),
            P("dp", "expert"),
            P("dp", "expert"),
            P("dp", "expert"),
            P(None, "expert", "dp"),
            P("expert", None),
        ),
        check_vma=False,
    )
```

```python
import functools

import jax
import jax.numpy as jnp
from jax import lax
from jax.experimental import pallas as pl
from jax.experimental.pallas import tpu as pltpu
from jax.sharding import PartitionSpec as P

HD = 128
BLOCK = 128

BETA_ONE = 0.9
BETA_TWO = 0.95
LEARN = 0.01
DECAY = 0.1
EPSILON = 1e-08
LIMIT = 448.0
CORRECT_ONE = 1.0 - 0.9**10
CORRECT_TWO = 1.0 - 0.95**10

ROWS = 96
KROWS = 32
HALF = 1024
KCOLS = 512
FOLD = 2 * ROWS
KFOLD = 16

BF = jnp.bfloat16
F32 = jnp.float32
VMEM_BYTES = 7 * 1024 * 1024
SLOTS = 6


def dp_of(x, y, c):
    return ((x % 2) * 4 + (y % 4)) * 2 + c % 2


def dp_perm(dx, dy, dc):
    return [
        (dp_of(x, y, c), dp_of(x + dx, y + dy, c + dc))
        for x in range(2)
        for y in range(4)
        for c in range(2)
    ]


def send(value, dx, dy, dc):
    return lax.ppermute(value, "dp", dp_perm(dx, dy, dc))


def ring(value):
    pairs = [
        (dp_of(x, y, c), dp_of(x, y + 1 - 2 * c, c))
        for x in range(2)
        for y in range(4)
        for c in range(2)
    ]
    return lax.ppermute(value, "dp", pairs)


def adam_update(param, moment, second, grad):
    moment = BETA_ONE * moment + (1.0 - BETA_ONE) * grad
    second = BETA_TWO * second + (1.0 - BETA_TWO) * grad * grad
    corrected = moment / CORRECT_ONE / (jnp.sqrt(second / CORRECT_TWO) + EPSILON)
    return (param * (1.0 - LEARN * DECAY) - LEARN * corrected, moment, second)


def to_grid(weights, scales):
    return jnp.clip(weights / scales, -LIMIT, LIMIT).astype(BF)


def owner(role, dx, x, y, c):
    step = {"far": 2, "near": 1 - 2 * c, "plain": 1 - 2 * c, "own": 0}[role]
    return dp_of(x + dx, y + 4 + step, 1 - c if role == "plain" else c)


def parts_of(batch, role, x, y, c, ep, kp, out):
    block = owner(role, 1 if batch == "turn" else 0, x, y, c)
    parts = [
        (ep.at[block, :, pl.ds(half * HALF, HALF)], out.at[pl.ds(half * ROWS, ROWS)])
        for half in range(2)
    ]
    if batch == "turn":
        for place, dx in enumerate((1, 0)):
            block = owner(role, dx, x, y, c)
            target = out.at[pl.ds(FOLD + place * KFOLD, KFOLD)]
            parts += [
                (kp.at[block, pl.ds(part * KFOLD, KFOLD)], target.at[:, pl.ds(part * KCOLS, KCOLS)])
                for part in range(2)
            ]
    return parts


def rows_of(batch):
    return FOLD + 2 * KFOLD if batch == "turn" else FOLD


def load_kernel(batch, roles, n_late, ep, kp, *refs):
    refs = refs[n_late:]
    n = len(roles)
    casts, keeps, buffer, sems = refs[:n], refs[n : 2 * n], refs[2 * n], refs[2 * n + 1]
    dp_index = lax.axis_index("dp")
    x, y, c = dp_index // 8, dp_index // 2 % 4, dp_index % 2
    work = [(role, 1 - c, out) for role, out in zip(roles, casts)]
    work += [(role, c, out) for role, out in zip(roles, keeps)]

    def start(index):
        role, core, _ = work[index]
        slot = index % SLOTS
        copies = [
            pltpu.make_async_copy(source, target, sems.at[slot, number])
            for number, (source, target) in enumerate(
                parts_of(batch, role, x, y, core, ep, kp, buffer.at[slot])
            )
        ]
        for copy in copies:
            copy.start()
        return copies

    flying = [start(index) for index in range(min(SLOTS, len(work)))]
    for index, (_, _, out) in enumerate(work):
        for copy in flying[index]:
            copy.wait()
        slot = index % SLOTS

        def rows(step, carry):
            some = pl.ds(pl.multiple_of(step * 16, 16), 16)
            out[0, some] = buffer[slot, some].astype(BF)
            return carry

        lax.fori_loop(0, rows_of(batch) // 16, rows, 0)
        if index + SLOTS < len(work):
            flying.append(start(index + SLOTS))


def load(ep, kp, batch, roles, late=()):
    shape = (1, rows_of(batch), HALF)
    vmem = pl.BlockSpec(memory_space=pltpu.VMEM)
    hbm = pl.BlockSpec(memory_space=pltpu.HBM)
    anywhere = pl.BlockSpec(memory_space=pl.ANY)
    out = pl.pallas_call(
        functools.partial(load_kernel, batch, roles, len(late)),
        out_shape=[jax.ShapeDtypeStruct(shape, BF)] * (2 * len(roles)),
        in_specs=[hbm, hbm] + [anywhere] * len(late),
        out_specs=[vmem] * (2 * len(roles)),
        scratch_shapes=[
            pltpu.VMEM((SLOTS,) + shape[1:], F32),
            pltpu.SemaphoreType.DMA((SLOTS, 6)),
        ],
        compiler_params=pltpu.CompilerParams(vmem_limit_bytes=VMEM_BYTES),
        cost_estimate=pl.CostEstimate(flops=1000, bytes_accessed=1000, transcendentals=0),
    )(ep, kp, *late)
    return out[: len(roles)], out[len(roles) :]


def plus(*values):
    total = values[0].astype(F32)
    for value in values[1:]:
        total = total + value.astype(F32)
    return total


def update_kernel(*refs):
    terms, (param, moment, variance, scales), results, grid = refs[:5], refs[5:9], refs[9:12], refs[12]
    start = lax.axis_index("dp") * ROWS
    low = start // BLOCK
    expert = lax.axis_index("expert")
    row = lax.broadcasted_iota(jnp.int32, (ROWS, 16), 0) + start
    row_scales = jnp.where(
        row < (low + 1) * BLOCK,
        scales[expert, pl.ds(low, 1), :],
        scales[expert, pl.ds(jnp.minimum(low + 1, 11), 1), :],
    )
    for j in range(8):
        for h in range(2):
            k = 2 * j + h
            columns = pl.ds(k * BLOCK, BLOCK)
            held = pl.ds(k % 8 * BLOCK, BLOCK)
            rows = pl.ds(k // 8 * ROWS, ROWS)
            grad = terms[0][0, rows, held].astype(F32)
            for term in terms[1:3]:
                grad = grad + term[0, rows, held].astype(F32)
            grad = grad + terms[3 + k // 8][0, :ROWS, held].astype(F32)
            new = adam_update(param[0, :, columns], moment[0, :, columns], variance[0, :, columns], grad)
            for result, value in zip(results, new):
                result[0, :, columns] = value
            grid[j, :, pl.ds(h * BLOCK, BLOCK)] = to_grid(new[0], row_scales[:, k : k + 1])


def key_kernel(own, arrived, param, moment, variance, scales, *results):
    quarter = lax.axis_index("dp") * KROWS // BLOCK
    row_scales = scales[pl.ds(quarter, 1), :]
    for part in range(2):
        rows = pl.ds(part * KFOLD, KFOLD)
        for k in range(KCOLS // BLOCK):
            columns = pl.ds(k * BLOCK, BLOCK)
            held = pl.ds(part * KCOLS + k * BLOCK, BLOCK)
            grad = own[0, FOLD + KFOLD :, held] + arrived[0, ROWS:, held].astype(F32)
            new = adam_update(param[rows, columns], moment[rows, columns], variance[rows, columns], grad)
            for result, value in zip(results, new):
                result[rows, columns] = value
            results[3][rows, columns] = to_grid(new[0], row_scales[:, k : k + 1])


def update(kernel, terms, param, moment, variance, scales, grid_shape):
    vmem = pl.BlockSpec(memory_space=pltpu.VMEM)
    near = lambda v: pltpu.with_memory_space_constraint(v, pltpu.VMEM)
    return pl.pallas_call(
        kernel,
        out_shape=[jax.ShapeDtypeStruct(param.shape, F32)] * 3 + [jax.ShapeDtypeStruct(grid_shape, BF)],
        in_specs=[vmem] * (len(terms) + 4),
        out_specs=[vmem] * 4,
        compiler_params=pltpu.CompilerParams(vmem_limit_bytes=VMEM_BYTES),
        cost_estimate=pl.CostEstimate(flops=1000, bytes_accessed=1000, transcendentals=0),
    )(*terms, near(param), near(moment), near(variance), scales)


def on_device(
    expert_partials,
    key_partials,
    expert_param,
    expert_moment,
    expert_second,
    key_param,
    key_moment,
    key_second,
    expert_scales,
    key_scales,
    rotary_order,
    expert_slot,
):
    dp_index = lax.axis_index("dp")
    x, y, c = dp_index // 8, dp_index // 2 % 4, dp_index % 2
    expert_partials, x, y, c = lax.optimization_barrier((expert_partials, x, y, c))
    ep = pltpu.with_memory_space_constraint(expert_partials.reshape(16, ROWS, 2 * HALF), pltpu.HBM)
    kp = pltpu.with_memory_space_constraint(key_partials.reshape(16, KROWS, KCOLS), pltpu.HBM)

    across = lambda values: [send(value, 0, 0, 1) for value in values]
    casts, keeps = load(ep, kp, "turn", ["far", "plain", "near"])
    got = across(casts)
    casts_b, keeps_b = load(ep, kp, "turn", ["own"], late=(casts[0],))
    got_b = across(casts_b)
    casts_c, keeps_c = load(ep, kp, "stay", ["far", "plain", "near", "own"], late=(casts_b[0],))
    got_c = across(casts_c)
    far = ring(plus(keeps[0], got[0]).astype(BF))
    plain = ring(plus(keeps[1], got[1]).astype(BF))
    near = ring(plus(keeps[2], got[2], far).astype(BF))
    cross = send(plain, 0, 0, 1)
    far_c = ring(plus(keeps_c[0], got_c[0]).astype(BF))
    plain_c = ring(plus(keeps_c[1], got_c[1]).astype(BF))
    turned = plus(keeps_b[0], got_b[0], cross, near)
    x_late = send(turned[:, :ROWS].astype(BF), 1, 0, 0)
    x_last = send(turned[:, ROWS : FOLD + KFOLD].astype(BF), 1, 0, 0)
    near_c = ring(plus(keeps_c[2], got_c[2], far_c).astype(BF))
    cross_c = send(plain_c, 0, 0, 1)
    stayed = plus(keeps_c[3], got_c[3]).astype(BF)
    new_kp, new_km, new_ks, key_grid = update(
        key_kernel,
        (turned, x_last),
        key_param,
        key_moment,
        key_second,
        key_scales,
        (KROWS, KCOLS),
    )
    key_grid, x_late = lax.optimization_barrier((key_grid, x_late))
    chip_x = send(key_grid, 1, 0, 0)
    new_ep, new_em, new_es, blocks = update(
        update_kernel,
        (stayed, cross_c, near_c, x_late, x_last),
        expert_param,
        expert_moment,
        expert_second,
        expert_scales,
        (8, ROWS, 256),
    )
    column = jnp.stack([key_grid, chip_x])
    column, blocks = lax.optimization_barrier((column, blocks))
    arrived = lax.all_to_all(blocks, "expert", split_axis=0, concat_axis=0, tiled=True)
    all_y = [column] + [send(column, 0, -step, 0) for step in (1, 2, 3)]
    all_y, arrived = lax.optimization_barrier((all_y, arrived))
    all_y = jnp.stack(all_y)
    everything = jnp.stack([all_y, send(all_y, 0, 0, 1)]).reshape(16 * KROWS, KCOLS)
    order = jnp.arange(16 * KROWS, dtype=jnp.int32)
    piece, row = order // KROWS, order % KROWS
    held = dp_of(x + piece % 2, y + piece // 2 % 4, c + piece // 8) * KROWS + row
    head = jnp.arange(HD, dtype=jnp.int32)
    goes = jnp.sum(jnp.where(rotary_order[:, None] == head[None, :], head[:, None], 0), axis=0)
    target = held // HD * HD + jnp.sum(
        jnp.where((held % HD)[:, None] == head[None, :], goes[None, :], 0), axis=1
    )
    pick = (target[:, None] == order[None, :]).astype(BF)
    server_key = lax.dot_general(
        everything, pick, (((0,), (0,)), ((), ())), preferred_element_type=F32
    ).astype(BF)
    placed = jnp.zeros_like(arrived).at[expert_slot].set(arrived)
    server_expert = jnp.transpose(placed, (0, 2, 1))
    return (new_ep, new_em, new_es, new_kp, new_km, new_ks, server_expert, server_key)


def solution(mesh):
    return jax.shard_map(
        on_device,
        mesh=mesh,
        in_specs=(
            P("dp", "expert", None, None),
            P("dp", None, "expert"),
            P("expert", "dp", None),
            P("expert", "dp", None),
            P("expert", "dp", None),
            P("dp", "expert"),
            P("dp", "expert"),
            P("dp", "expert"),
            P(),
            P(None, "expert"),
            P(),
            P(),
        ),
        out_specs=(
            P("expert", "dp", None),
            P("expert", "dp", None),
            P("expert", "dp", None),
            P("dp", "expert"),
            P("dp", "expert"),
            P("dp", "expert"),
            P(None, "expert", "dp"),
            P("expert", None),
        ),
        check_vma=False,
    )
```
